32 devices in a mesh: leaf: 4 (over z), row: 4 (over y, x), col: 2 (over core).
Axes of the slice: x: 2, y: 2, z: 4, core: 2. Of those that a mesh axis runs over, the one named last changes fastest.
Arguments:
- leaf_rhs: bfloat16 [8192, 1024], P(('leaf', 'col'), 'row'), may hold values from -6 to 6
- leaf_inverse: bfloat16 [8192, 2048], P('leaf', 'col'), may hold values from -0.125 to 0.125
- leaf_below: bfloat16 [8192, 2048], P('leaf', 'col'), may hold values from -0.0625 to 0.0625
- leaf_rows: int32 [4, 16], P('leaf'), may hold values from 16 to 63, as said below
- sep_rhs: bfloat16 [8192, 1024], P(('leaf', 'col'), 'row'), may hold values from -6 to 6
- sep_inverse: bfloat16 [8192, 2048], P('leaf', 'col'), may hold values from -0.125 to 0.125
- sep_below: bfloat16 [4096, 2048], P('leaf', 'col'), may hold values from -0.0625 to 0.0625
- sep_rows: int32 [4, 8], P('leaf'), may hold values from 16 to 63, as said below
- sep_width: int32 [4], replicated, may hold values from 1024 to 2048, as said below
Outputs:
- leaf_solution: bfloat16 [8192, 1024], P(('leaf', 'col'), 'row')
- sep_solution: bfloat16 [8192, 1024], P(('leaf', 'col'), 'row')
The draws below stay inside these ranges and needn't reach their ends.
Inputs may be any that keep to these rules, and one draw needn't show every extreme that they name: `sep_width`: multiples of 128; slot 4 / 2 (the root) has 2048; entry 0 is not used. `leaf_rows`: row i holds 16 different block rows a * 16 + p of the ancestors a of subtree i, with p * 128 < sep_width[a]. `sep_rows`: row a, for a slot a below the root, holds 8 different block rows b * 16 + p of the slots b at higher levels on the path from a to the root, with p * 128 < sep_width[b]; rows 0 and 2 are not used.
All inputs are finite; a program needn't handle non-finite values.
Results may differ from the reference program's by a relative error of at most 0.0065.
Values sent between devices are 32-bit elements; how exact they have to be, the bound alone decides.
No kernel may reach another device: no remote copies, remote signals or barrier semaphores. Data moves between devices by JAX's collectives and lax.ppermute only.
A program may use at most 128 MiB of HBM per device.

```python
import jax
import jax.numpy as jnp
from jax import lax

WSEP = 2048
WLEAF = 2048
PANEL = 128
RPAN = 8
RLEAF = 16
RHS = 1024
LEVELS = 2
N_LEAF = 4


def widths_of(key):
    base_key = jax.random.fold_in(key, 11)
    counts_now = jax.random.randint(base_key, (N_LEAF,), RPAN, WSEP // PANEL + 1)
    counts_now = counts_now.at[1].set(RPAN)
    counts_now = counts_now.at[N_LEAF - 1].set(WSEP // PANEL)
    counts_now = counts_now.at[N_LEAF // 2].set(WSEP // PANEL)
    return (counts_now * PANEL).astype(jnp.int32)


def pick_rows(key, node_idx, own_level, count_rows, salt):
    sep_panels = WSEP // PANEL
    widths = widths_of(key)
    level_idx = jnp.arange(1, LEVELS + 1, dtype=jnp.int32)
    span_all = 2 ** level_idx
    ancestor = node_idx[:, None] - node_idx[:, None] % span_all[None, :] + span_all[None, :] // 2
    live_panels = widths[ancestor] // PANEL
    panel_idx = jnp.arange(sep_panels, dtype=jnp.int32)
    panel_ids = ancestor[:, :, None] * sep_panels + panel_idx[None, None, :]
    valid = (panel_idx[None, None, :] < live_panels[:, :, None]) & (level_idx[None, :, None] > own_level[:, None, None])
    raw_scores = jax.random.randint(jax.random.fold_in(key, salt), (N_LEAF, LEVELS, sep_panels), 0, 2 ** 16)
    position = jnp.arange(LEVELS * sep_panels, dtype=jnp.int32).reshape(LEVELS, sep_panels)
    scores = raw_scores * (LEVELS * sep_panels) + position[None, :, :]
    first_level = level_idx[None, :, None] == 1
    forced_low = first_level & (panel_idx[None, None, :] == 0)
    forced_high = first_level & (panel_idx[None, None, :] == live_panels[:, :, None] - 1)
    scores = jnp.where(forced_low, -2, scores)
    scores = jnp.where(forced_high, -1, scores)
    scores = jnp.where(valid, scores, scores + 2 ** 28)
    flat_scores = scores.reshape(N_LEAF, LEVELS * sep_panels)
    flat_ids = panel_ids.reshape(N_LEAF, LEVELS * sep_panels)
    best_values, chosen = lax.top_k(-flat_scores, count_rows)
    return jnp.take_along_axis(flat_ids, chosen, axis=1).astype(jnp.int32)


def draw_sep_width(key, part):
    return widths_of(key)


def draw_leaf_rows(key, part):
    node_idx = jnp.arange(N_LEAF, dtype=jnp.int32)
    return pick_rows(key, node_idx, jnp.zeros((N_LEAF,), jnp.int32), RLEAF, 21)


def draw_sep_rows(key, part):
    node_idx = jnp.arange(N_LEAF, dtype=jnp.int32)
    depth_now = jnp.ones_like(node_idx)
    for bit_pos in range(1, LEVELS + 1):
        depth_now = depth_now + (node_idx % 2 ** bit_pos == 0).astype(jnp.int32)
    own_level = jnp.where((node_idx == 0) | (depth_now >= LEVELS), 0, depth_now)
    path_node = jnp.where(node_idx == N_LEAF // 2, N_LEAF - 1, node_idx).astype(jnp.int32)
    return pick_rows(key, path_node, own_level, RPAN, 37)


def levels(rng, extent, pieces, low, high):
    def one(dim, blocks):
        heights = jax.random.uniform(jax.random.fold_in(jax.random.fold_in(rng, 6), dim), (blocks,), jnp.float32, low / len(pieces), high / len(pieces))
        return jnp.repeat(jnp.exp(heights), extent[dim] // blocks).reshape((-1,) + (1,) * (len(extent) - dim - 1))

    gain = one(*pieces[0])
    for cut in pieces[1:]:
        gain = gain * one(*cut)
    return gain


def gaussian(stream_key, shape, scale, most, cuts=(), kind=jnp.bfloat16):
    factor_of = levels(stream_key, shape, cuts, -0.22, 0.18) if cuts else 1.0
    drawn = jax.random.normal(stream_key, shape, jnp.float32) * scale * factor_of
    return jnp.minimum(jnp.maximum(drawn, -most), most).astype(kind)


def setup_inputs(seed: int = 0) -> dict:
    splits = jax.random.split(jax.random.key(seed), 10)
    leaf_rhs = gaussian(splits[0], (N_LEAF * WLEAF, RHS), 1.0, 6.0, ((0, 8), (1, 4)))
    leaf_inverse = gaussian(splits[1], (N_LEAF * WLEAF, WLEAF), WLEAF ** -0.5, 0.125, ((0, 4), (1, 2)))
    leaf_below = gaussian(splits[2], (N_LEAF * RLEAF * PANEL, WLEAF), (4 * WLEAF) ** -0.5, 0.0625, ((0, 4), (1, 2)))
    leaf_rows = draw_leaf_rows(jax.random.fold_in(splits[9], 71), 0)
    sep_rhs = gaussian(splits[4], (N_LEAF * WSEP, RHS), 1.0, 6.0, ((0, 8), (1, 4)))
    sep_inverse = gaussian(splits[5], (N_LEAF * WSEP, WSEP), WSEP ** -0.5, 0.125, ((0, 4), (1, 2)))
    sep_below = gaussian(splits[6], (N_LEAF * RPAN * PANEL, WSEP), (4 * WSEP) ** -0.5, 0.0625, ((0, 4), (1, 2)))
    sep_rows = draw_sep_rows(jax.random.fold_in(splits[9], 71), 0)
    sep_width = draw_sep_width(jax.random.fold_in(splits[9], 71), 0)
    return dict(leaf_rhs=leaf_rhs, leaf_inverse=leaf_inverse, leaf_below=leaf_below, leaf_rows=leaf_rows, sep_rhs=sep_rhs, sep_inverse=sep_inverse, sep_below=sep_below, sep_rows=sep_rows, sep_width=sep_width)


def unit_lower(matrix):
    size_now = matrix.shape[0]
    return jnp.tril(matrix, -1) + jnp.eye(size_now, dtype=matrix.dtype)


def reference(leaf_rhs, leaf_inverse, leaf_below, leaf_rows, sep_rhs, sep_inverse, sep_below, sep_rows, sep_width):
    sep_panels = WSEP // PANEL
    leaf_height = RLEAF * PANEL
    sep_height = RPAN * PANEL
    pending = jnp.zeros((N_LEAF * sep_panels, PANEL, RHS), jnp.float32)
    leaf_parts = []
    for leaf_now in range(N_LEAF):
        right_side = leaf_rhs[leaf_now * WLEAF:(leaf_now + 1) * WLEAF]
        inverse = unit_lower(leaf_inverse[leaf_now * WLEAF:(leaf_now + 1) * WLEAF])
        solution = jnp.dot(inverse, right_side, preferred_element_type=jnp.float32).astype(jnp.bfloat16)
        leaf_parts.append(solution)
        below_now = leaf_below[leaf_now * leaf_height:(leaf_now + 1) * leaf_height]
        update = jnp.dot(below_now, solution, preferred_element_type=jnp.float32).reshape(RLEAF, PANEL, RHS)
        pending = pending.at[leaf_rows[leaf_now]].add(update)
    sep_parts = [jnp.zeros((WSEP, RHS), jnp.bfloat16) for slot_now in range(N_LEAF)]
    columns = jnp.arange(WSEP)
    for level_now in range(1, LEVELS + 1):
        span_now = 2 ** level_now
        for slot_now in range(span_now // 2, N_LEAF, span_now):
            block_now = pending[slot_now * sep_panels:(slot_now + 1) * sep_panels].reshape(WSEP, RHS)
            residual = (sep_rhs[slot_now * WSEP:(slot_now + 1) * WSEP].astype(jnp.float32) - block_now).astype(jnp.bfloat16)
            inverse = unit_lower(sep_inverse[slot_now * WSEP:(slot_now + 1) * WSEP])
            product = jnp.dot(inverse, residual, preferred_element_type=jnp.float32)
            solution = jnp.where(columns[:, None] < sep_width[slot_now], product, 0.0).astype(jnp.bfloat16)
            sep_parts[slot_now] = solution
            if level_now < LEVELS:
                below_now = sep_below[slot_now * sep_height:(slot_now + 1) * sep_height]
                update = jnp.dot(below_now, solution, preferred_element_type=jnp.float32).reshape(RPAN, PANEL, RHS)
                pending = pending.at[sep_rows[slot_now]].add(update)
    return jnp.concatenate(leaf_parts, 0), jnp.concatenate(sep_parts, 0)
```

```python
import functools

import jax
import jax.numpy as jnp
from jax import lax
from jax.experimental import pallas as pl
from jax.experimental.pallas import tpu as pltpu
from jax.sharding import PartitionSpec as P

PANEL = 128
TILE = 256
TAGS = 128
F32 = jnp.float32
BF16 = jnp.bfloat16
ANY = pl.BlockSpec(memory_space=pl.ANY)
VMEM = pl.BlockSpec(memory_space=pltpu.VMEM)
SMEM = pl.BlockSpec(memory_space=pltpu.SMEM)


def dot(left, right):
    return jnp.dot(left, right, preferred_element_type=F32)


def call(body, ins, specs, outs, out_specs, scratch=(), flops=0, moved=0):
    return pl.pallas_call(
        body,
        out_shape=outs,
        in_specs=specs,
        out_specs=out_specs,
        scratch_shapes=list(scratch),
        compiler_params=pltpu.CompilerParams(vmem_limit_bytes=40 * 2**20),
        cost_estimate=pl.CostEstimate(flops=flops, bytes_accessed=moved, transcendentals=0),
    )(*ins)


def shape(rows, cols, kind=F32):
    return jax.ShapeDtypeStruct((rows, cols), kind)


def masked_diag(tile):
    rows_here = lax.broadcasted_iota(jnp.int32, tile.shape, 0)
    cols_here = lax.broadcasted_iota(jnp.int32, tile.shape, 1)
    wide = tile.astype(F32)
    wide = jnp.where(rows_here > cols_here, wide, 0.0)
    return jnp.where(rows_here == cols_here, 1.0, wide).astype(BF16)


def lower_rows(read, rhs, tile_idx):
    lo, hi = tile_idx * TILE, (tile_idx + 1) * TILE
    total = dot(masked_diag(read(lo, hi, lo, hi)), rhs[lo:hi])
    if tile_idx:
        total = total + dot(read(lo, hi, 0, lo), rhs[0:lo])
    return total


def bottom_kernel(piece, inverse, rhs, out, buf, sems):
    steps = piece // TILE
    copies = [
        pltpu.make_async_copy(
            inverse.at[pl.ds(piece + t * TILE, TILE)], buf.at[pl.ds(t * TILE, TILE)], sems.at[t]
        )
        for t in range(steps)
    ]
    for one in copies:
        one.start()
    right = rhs[...]
    for t in range(steps):
        copies[t].wait()
        out[t * TILE : (t + 1) * TILE] = dot(buf[t * TILE : (t + 1) * TILE], right)


def key_of(row, levels, sep_panels):
    slot = row // sep_panels
    zeros = jnp.int32(0)
    for bit_pos in range(1, levels + 1):
        zeros = zeros + jnp.where(slot % 2**bit_pos == 0, 1, 0)
    return jnp.where(zeros == 0, levels - 1, zeros - 1) * sep_panels + row % sep_panels


def diagonal_kernel(piece, levels, sep_panels, inverse, rhs, leaf_rows, sep_rows, out, tags, buf, sems):
    steps = piece // TILE
    start = pl.multiple_of(lax.axis_index("col") * piece, piece)
    copies = [
        pltpu.make_async_copy(
            inverse.at[pl.ds(start + t * TILE, TILE)], buf.at[pl.ds(t * TILE, TILE)], sems.at[t]
        )
        for t in range(steps)
    ]
    for one in copies:
        one.start()
    n_leaf, n_sep = leaf_rows.shape[1], sep_rows.shape[1]
    keys = [key_of(leaf_rows[0, j], levels, sep_panels) for j in range(n_leaf)]
    for j in range(n_leaf):
        rank = jnp.int32(0)
        for i in range(n_leaf):
            if i != j:
                rank = rank + jnp.where(keys[i] < keys[j], 1, 0)
        tags[0, rank] = keys[j]
        tags[0, n_leaf + n_sep + rank] = jnp.int32(j)
    for j in range(n_sep):
        tags[0, n_leaf + j] = key_of(sep_rows[0, j], levels, sep_panels)
    right = rhs[...]
    for t in range(steps):
        copies[t].wait()
        out[t * TILE : (t + 1) * TILE] = lower_rows(lambda a, b, c, d: buf[a:b, c:d], right, t)


def below_kernel(first, j0, j1, order_at, *refs):
    if first:
        diag, other, below, tags, sol, keep, send, buf, sems = refs
    else:
        sol, below, tags, keep, send, buf, sems = refs
    copies = []
    for j in range(j0, j1):
        source = pl.multiple_of(tags[0, order_at + j] * PANEL, PANEL)
        copies.append(
            pltpu.make_async_copy(
                below.at[pl.ds(source, PANEL)], buf.at[pl.ds((j - j0) * PANEL, PANEL)], sems.at[j - j0]
            )
        )
    for one in copies:
        one.start()
    if first:
        sol[...] = (diag[...] + other[...]).astype(BF16)
    right = sol[...]
    half = right.shape[1] // 2
    is_first = lax.axis_index("col") == 0
    for t in range(0, j1 - j0, 2):
        copies[t].wait()
        copies[t + 1].wait()
        both = dot(buf[t * PANEL : (t + 2) * PANEL], right)
        left_half, right_half = both[:, :half], both[:, half:]
        keep[t * PANEL : (t + 2) * PANEL] = jnp.where(is_first, left_half, right_half)
        send[t * PANEL : (t + 2) * PANEL] = jnp.where(is_first, right_half, left_half)


def relay_kernel(chunk, per_chunk, *refs):
    count = chunk + 1
    mine, theirs = refs[:count], refs[count : 2 * count]
    my_tags, their_tags, out = refs[2 * count :]
    out[...] = jnp.zeros_like(out)
    for group, tags in ((mine, my_tags), (theirs, their_tags)):
        for i in range(count * per_chunk):
            place = tags[0, i] - chunk * per_chunk

            @pl.when((place >= 0) & (place < per_chunk))
            def _():
                at = pl.ds(pl.multiple_of(place * PANEL, PANEL), PANEL)
                inside = i % per_chunk
                out[at] += group[i // per_chunk][inside * PANEL : (inside + 1) * PANEL]


def rest_kernel(n_compact, per_array, n_dense, base, *refs):
    arrays = refs[:n_compact]
    tags = refs[n_compact : 2 * n_compact]
    firsts = per_array
    dense = refs[2 * n_compact : 2 * n_compact + n_dense]
    out = refs[-1]
    panels = out.shape[0] // PANEL
    if n_dense:
        out[...] = dense[0][...] + dense[1][...]
    else:
        out[...] = jnp.zeros_like(out)
    for array, tag, (tag_at, count) in zip(arrays, tags, firsts):
        for i in range(count):
            place = tag[0, tag_at + i] - base

            @pl.when((place >= 0) & (place < panels))
            def _():
                at = pl.ds(pl.multiple_of(place * PANEL, PANEL), PANEL)
                out[at] += array[i * PANEL : (i + 1) * PANEL]


def narrow_kernel(wide, out):
    out[...] = wide[...].astype(BF16)


def solve_kernel(plan, *refs):
    refs = list(refs)

    def take(count):
        got = refs[:count]
        del refs[:count]
        return got

    compact = take(plan["n_compact"])
    tags = take(plan["n_compact"])
    dense = take(plan["n_dense"])
    rhs_mine, rhs_theirs, widths, inverse, from_top, from_bottom = take(6)
    below, from_below = take(2) if plan["update"] else (None, None)
    before = take(2) if plan["before"] else None
    keep, send = take(2)
    update = take(1)[0] if plan["update"] else None
    tri, acc, res, sol, sems = take(5)
    if plan["update"]:
        low, low_sems = take(2)
    piece = rhs_mine.shape[0]
    half = rhs_theirs.shape[1]
    is_first = lax.axis_index("col") == 0
    leaf = lax.axis_index("leaf")
    span = 2 ** plan["level"]
    is_owner = leaf % span == span // 2
    steps = piece // TILE

    def fetch(source, row0, buf, at, sem):
        return pltpu.make_async_copy(source.at[pl.ds(row0, TILE)], buf.at[at, pl.ds(row0 % piece, TILE)], sem)

    sources = ((inverse, 0, from_top, 0), (inverse, piece, from_bottom, 0), (from_bottom, 0, inverse, piece))
    for t in range(steps):
        for q, (src0, off0, src1, off1) in enumerate(sources):

            @pl.when(is_first)
            def _():
                fetch(src0, off0 + t * TILE, tri, q, sems.at[q, t]).start()

            @pl.when(jnp.logical_not(is_first))
            def _():
                fetch(src1, off1 + t * TILE, tri, q, sems.at[q, t]).start()

    if plan["update"]:
        low_steps = below.shape[0] // TILE
        for t in range(low_steps):
            for q, (src0, src1) in enumerate(((below, from_below), (from_below, below))):

                @pl.when(is_first)
                def _():
                    fetch(src0, t * TILE, low, q, low_sems.at[q, t]).start()

                @pl.when(jnp.logical_not(is_first))
                def _():
                    fetch(src1, t * TILE, low, q, low_sems.at[q, t]).start()

    @pl.when(is_first)
    def _():
        acc[0:piece] = rhs_mine[:, 0:half].astype(F32)
        acc[piece : 2 * piece] = rhs_theirs[...]

    @pl.when(jnp.logical_not(is_first))
    def _():
        acc[0:piece] = rhs_theirs[...]
        acc[piece : 2 * piece] = rhs_mine[:, half : 2 * half].astype(F32)

    pieces = len(dense) // 2
    at_row = 0
    for d in range(pieces):
        rows = min(dense[d].shape[0], 2 * piece - at_row)
        acc[at_row : at_row + rows] -= dense[d][0:rows] + dense[pieces + d][0:rows]
        at_row += rows
    panels = 2 * piece // PANEL
    for array, tag, (tag_at, count) in zip(compact, tags, plan["firsts"]):
        for i in range(count):
            place = tag[0, tag_at + i] - plan["base"]

            @pl.when((place >= 0) & (place < panels))
            def _():
                at = pl.ds(pl.multiple_of(place * PANEL, PANEL), PANEL)
                acc[at] -= array[i * PANEL : (i + 1) * PANEL]

    res[...] = acc[...].astype(BF16)
    slot = leaf - leaf % span + span // 2
    width = widths[slot]
    row_ids = lax.broadcasted_iota(jnp.int32, (TILE, half), 0)

    def finish(total, row0):
        total = jnp.where(row_ids + row0 < width, total, 0.0)
        acc[row0 : row0 + TILE] = total
        sol[row0 : row0 + TILE] = total.astype(BF16)

    upper, lower = res[0:piece], res[piece : 2 * piece]
    for t in range(steps):
        fetch(inverse, t * TILE, tri, 0, sems.at[0, t]).wait()
        finish(lower_rows(lambda a, b, c, d: tri[0, a:b, c:d], upper, t), t * TILE)
    for t in range(steps):
        fetch(inverse, t * TILE, tri, 1, sems.at[1, t]).wait()
        fetch(inverse, t * TILE, tri, 2, sems.at[2, t]).wait()
        total = lower_rows(lambda a, b, c, d: tri[2, a:b, c:d], lower, t)
        total = total + dot(tri[1, t * TILE : (t + 1) * TILE], upper)
        finish(total, piece + t * TILE)
    if plan["update"]:
        upper, lower = sol[0:piece], sol[piece : 2 * piece]
        for t in range(low_steps):
            fetch(below, t * TILE, low, 0, low_sems.at[0, t]).wait()
            fetch(below, t * TILE, low, 1, low_sems.at[1, t]).wait()
            at = slice(t * TILE, (t + 1) * TILE)
            update[at] = dot(low[0, at], upper) + dot(low[1, at], lower)
    kept_at = pl.ds(pl.multiple_of(lax.axis_index("col") * piece, piece), piece)
    sent_at = pl.ds(pl.multiple_of((1 - lax.axis_index("col")) * piece, piece), piece)

    @pl.when(is_owner)
    def _():
        keep[...] = acc[kept_at]
        send[...] = acc[sent_at]

    @pl.when(jnp.logical_not(is_owner))
    def _():
        if before is None:
            keep[...] = jnp.zeros_like(keep)
            send[...] = jnp.zeros_like(send)
        else:
            keep[...] = before[0][...]
            send[...] = before[1][...]


def join_kernel(keep, other, out):
    half = keep.shape[1]
    is_first = lax.axis_index("col") == 0

    @pl.when(is_first)
    def _():
        out[:, 0:half] = keep[...].astype(BF16)
        out[:, half : 2 * half] = other[...].astype(BF16)

    @pl.when(jnp.logical_not(is_first))
    def _():
        out[:, 0:half] = other[...].astype(BF16)
        out[:, half : 2 * half] = keep[...].astype(BF16)


def on_device(
    leaf_rhs, leaf_inverse, leaf_below, leaf_rows, sep_rhs, sep_inverse, sep_below, sep_rows, sep_width
):
    leaves = lax.axis_size("leaf")
    levels = leaves.bit_length() - 1
    piece, width_rhs = leaf_rhs.shape
    half = width_rhs // 2
    sep_cols = sep_inverse.shape[0]
    sep_piece = sep_inverse.shape[1]
    sep_panels = sep_cols // PANEL
    n_leaf, n_sep = leaf_rows.shape[1], sep_rows.shape[1]
    col = lax.axis_index("col")
    swap = [(0, 1), (1, 0)]

    steps = piece // TILE
    weights = 2 * piece * piece
    bottom = call(
        functools.partial(bottom_kernel, piece),
        (leaf_inverse, leaf_rhs),
        [ANY, VMEM],
        shape(piece, width_rhs),
        VMEM,
        [pltpu.VMEM((piece, piece), BF16), pltpu.SemaphoreType.DMA((steps,))],
        weights * width_rhs,
        weights,
    )
    from_left = lax.ppermute(bottom, "col", [(0, 1)])
    diag, tags = call(
        functools.partial(diagonal_kernel, piece, levels, sep_panels),
        (leaf_inverse, leaf_rhs, leaf_rows, sep_rows),
        [ANY, VMEM, SMEM, SMEM],
        (shape(piece, width_rhs), shape(1, TAGS, jnp.int32)),
        (VMEM, SMEM),
        [pltpu.VMEM((piece, piece), BF16), pltpu.SemaphoreType.DMA((steps,))],
        weights * width_rhs,
        weights,
    )

    per_chunk = 4
    n_chunks = n_leaf // per_chunk
    order_at = n_leaf + n_sep

    def below(first, j0, j1, ins):
        rows = (j1 - j0) * PANEL
        outs = (shape(rows, half), shape(rows, half))
        specs = [VMEM, VMEM, ANY, SMEM] if first else [VMEM, ANY, SMEM]
        if first:
            outs = (shape(piece, width_rhs, BF16),) + outs
        return call(
            functools.partial(below_kernel, first, j0, j1, order_at),
            ins,
            specs,
            outs,
            (VMEM,) * len(outs),
            [pltpu.VMEM((rows, piece), BF16), pltpu.SemaphoreType.DMA((j1 - j0,))],
            2 * rows * piece * width_rhs,
            2 * rows * piece,
        )

    leaf_solution, keep0, send0 = below(True, 0, per_chunk, (diag, from_left, leaf_below, tags))
    mine = [keep0 + lax.ppermute(send0, "col", swap)]
    keep1, send1 = below(False, per_chunk, n_leaf, (leaf_solution, leaf_below, tags))
    got1 = lax.ppermute(send1, "col", swap)
    for chunk in range(1, n_chunks):
        at = slice((chunk - 1) * per_chunk * PANEL, chunk * per_chunk * PANEL)
        mine.append(keep1[at] + got1[at])

    up = [(i, i + 1) for i in range(0, leaves, 2)]
    their_tags = lax.ppermute(tags, "leaf", up)
    theirs = [lax.ppermute(one, "leaf", up) for one in mine]

    rhs_out = jnp.where(col == 0, sep_rhs[:, half:], sep_rhs[:, :half]).astype(F32)
    rhs_theirs = lax.ppermute(rhs_out, "col", swap)

    def narrow(wide):
        return call(narrow_kernel, (wide,), [VMEM], shape(*wide.shape, BF16), VMEM, (), 0, 6 * wide.size)

    from_bottom = narrow(lax.ppermute(sep_inverse[sep_piece:].astype(F32), "col", swap))
    from_top = narrow(lax.ppermute(sep_inverse[:sep_piece].astype(F32), "col", [(0, 1)]))
    from_below = narrow(lax.ppermute(sep_below.astype(F32), "col", swap))

    dense = []
    for chunk in range(n_chunks):
        dense.append(
            call(
                functools.partial(relay_kernel, chunk, per_chunk),
                (*mine[: chunk + 1], *theirs[: chunk + 1], tags, their_tags),
                [VMEM] * (2 * chunk + 2) + [SMEM] * 2,
                shape(per_chunk * PANEL, half),
                VMEM,
                (),
                0,
                3 * per_chunk * PANEL * half * 4,
            )
        )
    chunk_firsts = [(c * per_chunk, per_chunk) for c in range(n_chunks)] * 2

    def rest(base, arrays, tag_list, firsts, parts):
        rows = (levels - 1) * sep_cols - base * PANEL
        if not rows:
            return None
        return call(
            functools.partial(rest_kernel, len(arrays), firsts, len(parts), base),
            (*arrays, *tag_list, *parts),
            [VMEM] * len(arrays) + [SMEM] * len(tag_list) + [VMEM] * len(parts),
            shape(rows, half),
            VMEM,
        )

    def solve(level, arrays, tag_list, firsts, parts, base, before):
        update = level < levels
        plan = dict(
            level=level,
            n_compact=len(arrays),
            n_dense=len(parts),
            firsts=firsts,
            base=base,
            update=update,
            before=before is not None,
        )
        ins = [*arrays, *tag_list, *parts, sep_rhs, rhs_theirs, sep_width, sep_inverse, from_top, from_bottom]
        specs = [VMEM] * len(arrays) + [SMEM] * len(tag_list) + [VMEM] * (len(parts) + 2) + [SMEM] + [ANY] * 3
        outs = [shape(sep_piece, half), shape(sep_piece, half)]
        scratch = [
            pltpu.VMEM((3, sep_piece, sep_piece), BF16),
            pltpu.VMEM((sep_cols, half), F32),
            pltpu.VMEM((sep_cols, half), BF16),
            pltpu.VMEM((sep_cols, half), BF16),
            pltpu.SemaphoreType.DMA((3, sep_piece // TILE)),
        ]
        if update:
            ins += [sep_below, from_below]
            specs += [ANY] * 2
            outs.append(shape(sep_below.shape[0], half))
            scratch += [
                pltpu.VMEM((2, sep_below.shape[0], sep_piece), BF16),
                pltpu.SemaphoreType.DMA((2, sep_below.shape[0] // TILE)),
            ]
        if before is not None:
            ins += list(before)
            specs += [VMEM] * 2
        got = call(
            functools.partial(solve_kernel, plan),
            ins,
            specs,
            tuple(outs),
            (VMEM,) * len(outs),
            scratch,
            2 * sep_cols * sep_cols * half,
            2 * sep_cols * sep_cols,
        )
        return got[:2], got[2] if update else None

    compact, compact_tags = mine + theirs, [tags] * n_chunks + [their_tags] * n_chunks
    held, update = solve(
        1, compact, compact_tags, chunk_firsts, [], (levels - 1) * sep_panels, None
    )
    above = rest(sep_panels, compact, compact_tags, chunk_firsts, [])
    for level in range(2, levels + 1):
        span = 2**level
        owners = range(span // 2, leaves, span)
        step = span // 4
        lists = [[(a - step, a) for a in owners], [(a + step, a) for a in owners]]
        parts = dense + ([above] if above is not None else [])
        came = [[lax.ppermute(one, "leaf", pairs) for one in parts] for pairs in lists]
        came_tags = [lax.ppermute(tags, "leaf", pairs) for pairs in lists]
        came_update = [lax.ppermute(update, "leaf", pairs) for pairs in lists]
        firsts = [(n_leaf, n_sep)] * 2
        head = [one[: len(dense)] for one in came]
        base = (level - 2) * sep_panels
        held, update = solve(level, came_update, came_tags, firsts, head[0] + head[1], base, held)
        if level < levels:
            tails = [one[-1] for one in came]
            above = rest((level - 1) * sep_panels, came_update, came_tags, firsts, tails)
            dense, above = [above[:sep_cols]], above[sep_cols:] if level < levels - 1 else None
    other = lax.ppermute(held[1], "col", swap)
    sep_solution = call(join_kernel, (held[0], other), [VMEM] * 2, shape(sep_piece, width_rhs, BF16), VMEM)
    return leaf_solution, sep_solution


def solution(mesh):
    placed = (
        P(("leaf", "col"), "row"),
        P("leaf", "col"),
        P("leaf", "col"),
        P("leaf", None),
        P(("leaf", "col"), "row"),
        P("leaf", "col"),
        P("leaf", "col"),
        P("leaf", None),
        P(),
    )
    return jax.shard_map(
        on_device,
        mesh=mesh,
        in_specs=placed,
        out_specs=(P(("leaf", "col"), "row"), P(("leaf", "col"), "row")),
        check_vma=False,
    )
```

```python
import functools

import jax
import jax.numpy as jnp
from jax import lax
from jax.experimental import pallas as pl
from jax.experimental.pallas import tpu as pltpu
from jax.sharding import PartitionSpec as P

PANEL = 128
TILE = 256
TAGS = 128
COST = 1000
CUTS, PARTS = (0, 5, 9, 16), 16
VMEM_MIB = 8
LEAF_COST = 2 * 10**9
OWN_PART = 13
SPLIT = 4
PINNED = 2
BASE_COST = 10**12
F32 = jnp.float32
BF16 = jnp.bfloat16
ANY = pl.BlockSpec(memory_space=pl.ANY)
VMEM = pl.BlockSpec(memory_space=pltpu.VMEM)
SMEM = pl.BlockSpec(memory_space=pltpu.SMEM)
HBM = pl.BlockSpec(memory_space=pltpu.HBM)


def dot(left, right):
    return jnp.dot(left, right, preferred_element_type=F32)


def call(body, ins, specs, outs, out_specs, scratch=(), after=(), flops=COST, moved=1):
    count, extra = len(ins), len(after)

    def trimmed(*refs):
        body(*refs[:count], *refs[count + extra :])

    return pl.pallas_call(
        trimmed,
        out_shape=outs,
        in_specs=list(specs) + [ANY] * extra,
        out_specs=out_specs,
        scratch_shapes=list(scratch),
        compiler_params=pltpu.CompilerParams(vmem_limit_bytes=VMEM_MIB * 2**20),
        cost_estimate=pl.CostEstimate(flops=flops, bytes_accessed=moved, transcendentals=0),
    )(*ins, *after)


def shape(rows, cols, kind=F32):
    return jax.ShapeDtypeStruct((rows, cols), kind)


def masked_diag(tile):
    rows_here = lax.broadcasted_iota(jnp.int32, tile.shape, 0)
    cols_here = lax.broadcasted_iota(jnp.int32, tile.shape, 1)
    wide = tile.astype(F32)
    wide = jnp.where(rows_here > cols_here, wide, 0.0)
    return jnp.where(rows_here == cols_here, 1.0, wide).astype(BF16)


def lower_rows(read, rhs, tile_idx):
    lo, hi = tile_idx * TILE, (tile_idx + 1) * TILE
    total = dot(masked_diag(read(lo, hi, lo, hi)), rhs[lo:hi])
    if tile_idx:
        total = total + dot(read(lo, hi, 0, lo), rhs[0:lo])
    return total


def key_of(row, levels, sep_panels):
    slot = lax.div(row, jnp.int32(sep_panels))
    zeros = jnp.int32(0)
    for bit_pos in range(1, levels + 1):
        zeros = zeros + jnp.where(slot & (2**bit_pos - 1) == 0, 1, 0)
    return jnp.where(zeros == 0, levels - 1, zeros - 1) * sep_panels + row - slot * sep_panels


def tags_kernel(levels, sep_panels, leaf_rows, sep_rows, tags):
    n_leaf, n_sep = leaf_rows.shape[1], sep_rows.shape[1]
    keys = [key_of(leaf_rows[0, j], levels, sep_panels) for j in range(n_leaf)]
    ranks = [jnp.int32(0)] * n_leaf
    for j in range(n_leaf):
        for i in range(j):
            less = jnp.where(keys[i] < keys[j], 1, 0)
            ranks[j] = ranks[j] + less
            ranks[i] = ranks[i] + 1 - less
    for j in range(n_leaf):
        tags[0, ranks[j]] = keys[j]
        tags[0, n_leaf + n_sep + ranks[j]] = jnp.int32(j)
    for j in range(n_sep):
        tags[0, n_leaf + j] = key_of(sep_rows[0, j], levels, sep_panels)


def diagonal_kernel(piece, inverse, rhs, out):
    right = rhs[...]

    def product(first):
        for t in range(piece // TILE):
            out[t * TILE : (t + 1) * TILE] = lower_rows(lambda a, b, c, d: inverse[first + a : first + b, c:d], right, t)

    @pl.when(lax.axis_index("col") == 0)
    def _():
        product(0)

    @pl.when(lax.axis_index("col") != 0)
    def _():
        product(piece)


def leaf_sum(diag, other):
    return (diag[...] + jnp.where(lax.axis_index("col") == 0, 0.0, other[...])).astype(BF16)


def sum_kernel(diag, other, out, token):
    out[...] = leaf_sum(diag, other)
    token[...] = diag[0:8, 0:128]


def below_kernel(order_at, diag, other, below, tags, keep, send):
    right = leaf_sum(diag, other)
    half = keep.shape[1]
    is_first = lax.axis_index("col") == 0
    for t in range(keep.shape[0] // PANEL):
        source = pl.multiple_of(tags[0, order_at + t] * PANEL, PANEL)
        both = dot(below[pl.ds(source, PANEL)], right)
        left_half, right_half = both[:, :half], both[:, half:]
        keep[t * PANEL : (t + 1) * PANEL] = jnp.where(is_first, left_half, right_half)
        send[t * PANEL : (t + 1) * PANEL] = jnp.where(is_first, right_half, left_half)


def gather_kernel(firsts, keep, there, tags, *outs):
    chunks, owns = outs[: len(firsts)], outs[len(firsts) :]
    for chunk, (first, count) in zip(chunks, firsts):
        at = slice(first * PANEL, (first + count) * PANEL)
        chunk[...] = keep[at] + there[at]
    base = 0
    for own in owns:
        own[...] = jnp.zeros_like(own)
        add_rows(own, base, own.shape[0] // PANEL, chunks, [tags] * len(chunks), firsts, 1)
        base += own.shape[0] // PANEL


def add_rows(out, base, panels, arrays, tags, firsts, sign):
    for array, tag, (tag_at, count) in zip(arrays, tags, firsts):
        for i in range(count):
            place = tag[0, tag_at + i] - base

            @pl.when((place >= 0) & (place < panels))
            def _():
                at = pl.ds(pl.multiple_of(place * PANEL, PANEL), PANEL)
                rows = array[i * PANEL : (i + 1) * PANEL]
                out[at] = out[at] + rows if sign > 0 else out[at] - rows


def scatter_kernel(base, firsts, start, *refs):
    arrays, tags = refs[: len(firsts)], refs[len(firsts) : 2 * len(firsts)]
    dense = refs[2 * len(firsts) : -1]
    out = refs[-1]
    if not dense:
        out[...] = jnp.zeros_like(out)
    at, low, high = 0, start, start + out.shape[0]
    for one in dense:
        first, last = max(low - at, 0), min(high - at, one.shape[0])
        if first < last:
            out[at + first - low : at + last - low] = one[first:last]
        at += one.shape[0]
    add_rows(out, base, out.shape[0] // PANEL, arrays, tags, firsts, 1)


def base_kernel(base, firsts, n_dense, *refs):
    refs = list(refs)
    arrays, tags = refs[: len(firsts)], refs[len(firsts) : 2 * len(firsts)]
    dense = refs[2 * len(firsts) : 2 * len(firsts) + n_dense]
    mine, theirs, out = refs[2 * len(firsts) + n_dense :]
    piece, half = theirs.shape
    is_first = lax.axis_index("col") == 0

    @pl.when(is_first)
    def _():
        out[0:piece] = mine[:, 0:half].astype(F32)
        out[piece : 2 * piece] = theirs[...]

    @pl.when(jnp.logical_not(is_first))
    def _():
        out[0:piece] = theirs[...]
        out[piece : 2 * piece] = mine[:, half : 2 * half].astype(F32)

    at_row = 0
    for one in dense:
        rows = min(one.shape[0], 2 * piece)
        out[at_row : at_row + rows] -= one[0:rows]
        at_row = (at_row + rows) % (2 * piece)
    add_rows(out, base, 2 * piece // PANEL, arrays, tags, firsts, -1)


def residual_kernel(base, firsts, *refs):
    arrays, tags = refs[: len(firsts)], refs[len(firsts) : 2 * len(firsts)]
    right, keep, send, acc = refs[2 * len(firsts) :]
    acc[...] = right[...]
    add_rows(acc, base, acc.shape[0] // PANEL, arrays, tags, firsts, -1)
    piece = keep.shape[0]
    is_first = lax.axis_index("col") == 0

    @pl.when(is_first)
    def _():
        keep[...] = acc[0:piece]
        send[...] = acc[piece : 2 * piece]

    @pl.when(jnp.logical_not(is_first))
    def _():
        keep[...] = acc[piece : 2 * piece]
        send[...] = acc[0:piece]


def across_kernel(mine, theirs, inverse, right, *outs):
    piece, half = mine.shape
    is_first = lax.axis_index("col") == 0
    one, two = mine[...].astype(BF16), theirs[...].astype(BF16)
    right[:, 0:half] = jnp.where(is_first, one, two)
    right[:, half : 2 * half] = jnp.where(is_first, two, one)
    held = right[...]
    per = piece // len(outs)
    for t in range(piece // TILE):
        out, at = outs[t * TILE // per], t * TILE % per
        out[at : at + TILE] = dot(inverse[piece + t * TILE : piece + (t + 1) * TILE], held)


def finish_kernel(plan, *refs):
    refs = list(refs)

    def take(count):
        got = refs[:count]
        del refs[:count]
        return got

    diag = take(1)[0]
    others = take(plan["split"])
    widths = take(1)[0]
    below = take(1)[0] if plan["update"] else None
    before = take(1)[0] if plan["before"] else None
    out = take(1)[0]
    piece, half = out.shape[0], out.shape[1] // 2
    is_first = lax.axis_index("col") == 0
    leaf = lax.axis_index("leaf")
    span = 2 ** plan["level"]
    is_owner = leaf % span == span // 2
    width = widths[leaf - leaf % span + span // 2] - jnp.where(is_first, 0, piece)
    row_ids = lax.broadcasted_iota(jnp.int32, out.shape, 0)
    other = jnp.concatenate([one[...] for one in others], 0)
    total = diag[...] + jnp.where(is_first, 0.0, other)
    sol = jnp.where(row_ids < width, total, 0.0).astype(BF16)
    if plan["update"]:
        keep, *sends = take(1 + plan["split"])
        per = sends[0].shape[0]
        for t in range(0, below.shape[0], TILE):
            both = dot(below[t : t + TILE], sol)
            left_half, right_half = both[:, :half], both[:, half:]
            keep[t : t + TILE] = jnp.where(is_first, left_half, right_half)
            sends[t // per][t % per : t % per + TILE] = jnp.where(is_first, right_half, left_half)

    if before is None:
        out[...] = jnp.where(is_owner, sol, jnp.zeros_like(sol))
    else:
        out[...] = jnp.where(is_owner, sol, before[...])


def sum_two_kernel(one, two, out):
    out[...] = one[...] + two[...]


def sum_parts_kernel(whole, *refs):
    *parts, out = refs
    at = 0
    for part in parts:
        here = slice(at, at + part.shape[0])
        out[here] = whole[here] + part[...]
        at += part.shape[0]


def sum_two(one, two):
    return call(sum_two_kernel, (one, two), [VMEM] * 2, shape(*one.shape), VMEM)


def on_device(
    leaf_rhs, leaf_inverse, leaf_below, leaf_rows, sep_rhs, sep_inverse, sep_below, sep_rows, sep_width
):
    leaves = lax.axis_size("leaf")
    levels = leaves.bit_length() - 1
    piece, width_rhs = leaf_rhs.shape
    half = width_rhs // 2
    sep_cols = sep_inverse.shape[0]
    sep_piece = sep_inverse.shape[1]
    sep_panels = sep_cols // PANEL
    n_leaf, n_sep = leaf_rows.shape[1], sep_rows.shape[1]
    col = lax.axis_index("col")
    swap = [(0, 1), (1, 0)]

    bottom = dot(leaf_inverse[piece:], leaf_rhs)
    other = lax.ppermute(bottom, "col", swap)
    tags = call(
        functools.partial(tags_kernel, levels, sep_panels),
        (leaf_rows, sep_rows),
        [SMEM, SMEM],
        shape(1, TAGS, jnp.int32),
        SMEM,
        after=[bottom],
        flops=LEAF_COST,
    )
    diag = call(
        functools.partial(diagonal_kernel, piece),
        (leaf_inverse, leaf_rhs),
        [VMEM, VMEM],
        shape(piece, width_rhs),
        VMEM,
        after=[tags],
        flops=LEAF_COST,
    )

    tags_swap = lax.ppermute(tags, "leaf", [(i, i ^ 1) for i in range(leaves)])
    up = [(a - 1, a) for a in range(2, leaves, 4)]
    tags_up = lax.ppermute(tags, "leaf", up)

    rhs_out = jnp.where(col == 0, sep_rhs[:, half:], sep_rhs[:, :half]).astype(F32)
    rhs_theirs = lax.ppermute(rhs_out, "col", swap)

    starts = [n_leaf * part // PARTS for part in CUTS]
    counts = [(a, b - a) for a, b in zip(starts, starts[1:])]
    chunks = len(counts)
    keep, send = call(
        functools.partial(below_kernel, n_leaf + n_sep),
        (diag, other, leaf_below, tags),
        [VMEM] * 3 + [SMEM],
        (shape(n_leaf * PANEL, half),) * 2,
        (VMEM,) * 2,
        after=[rhs_theirs],
    )
    own_rows = sep_panels * OWN_PART // PARTS * PANEL
    got = call(
        functools.partial(gather_kernel, counts),
        (keep, lax.ppermute(send, "col", swap), tags),
        [VMEM] * 2 + [SMEM],
        (*(shape(count * PANEL, half) for first, count in counts), shape(own_rows, half), shape(sep_cols - own_rows, half)),
        (VMEM,) * (chunks + 2),
        after=[tags_swap],
    )
    mine, own = list(got[:chunks]), list(got[chunks:])

    theirs = [lax.ppermute(one, "leaf", [(i, i + 1) for i in range(0, leaves, 2)]) for one in mine]

    def scatter(rows, base, arrays, tag_list, firsts, dense, start, after):
        return call(
            functools.partial(scatter_kernel, base, firsts, start),
            (*arrays, *tag_list, *dense),
            [VMEM] * len(arrays) + [SMEM] * len(tag_list) + [VMEM] * len(dense),
            shape(rows, half),
            VMEM,
            after=after,
        )

    def right_side(base, arrays, tag_list, firsts, dense, after, flops=COST):
        return call(
            functools.partial(base_kernel, base, firsts, len(dense)),
            (*arrays, *tag_list, *dense, sep_rhs, rhs_theirs),
            [VMEM] * len(arrays) + [SMEM] * len(tag_list) + [VMEM] * (len(dense) + 2),
            shape(sep_cols, half),
            VMEM,
            after=after,
            flops=flops,
        )

    def solve(level, arrays, tag_list, firsts, base, right, before, after, after_late=(), split=1):
        update = level < levels
        keep, send = call(
            functools.partial(residual_kernel, base, firsts),
            (*arrays, *tag_list, right),
            [VMEM] * len(arrays) + [SMEM] * len(tag_list) + [VMEM],
            (shape(sep_piece, half),) * 2,
            (VMEM,) * 2,
            [pltpu.VMEM((sep_cols, half), F32)],
            after=after,
        )
        residual, *across = call(
            across_kernel,
            (keep, lax.ppermute(send, "col", swap), sep_inverse),
            [VMEM] * 3,
            (shape(sep_piece, width_rhs, BF16), *(shape(sep_piece // split, width_rhs),) * split),
            (VMEM,) * (1 + split),
        )
        other = [lax.ppermute(one, "col", swap) for one in across]
        diag = call(
            functools.partial(diagonal_kernel, sep_piece),
            (sep_inverse, residual),
            [VMEM] * 2,
            shape(sep_piece, width_rhs),
            VMEM,
        )
        plan = dict(level=level, update=update, before=before is not None, split=split)
        ins = [diag, *other, sep_width]
        outs = [shape(sep_piece, width_rhs, BF16)]
        if update:
            ins.append(sep_below)
            outs += [shape(sep_below.shape[0], half)] + [shape(sep_below.shape[0] // split, half)] * split
        if before is not None:
            ins.append(before)
        got = call(
            functools.partial(finish_kernel, plan),
            ins,
            [VMEM] * (1 + split) + [SMEM] + [VMEM] * (len(ins) - 2 - split),
            tuple(outs),
            (VMEM,) * len(outs),
        )
        if not update:
            return got[0], None
        there = [lax.ppermute(one, "col", swap) for one in got[2:]]
        total = call(
            sum_parts_kernel, (got[1], *there), [VMEM] * (1 + split), shape(*got[1].shape), VMEM, after=after_late
        )
        return got[0], total

    down = [(i + 1, i) for i in range(2, leaves, 4)]
    own_right = [lax.ppermute(one, "leaf", down) for one in own]
    right = right_side((levels - 1) * sep_panels, mine, [tags] * chunks, counts, [], own[:1])
    leaf_solution, last = call(
        sum_kernel,
        (diag, other),
        [VMEM] * 2,
        (shape(piece, width_rhs, BF16), shape(8, 128)),
        (VMEM, VMEM),
        after=[right],
    )

    came = []
    for n in range(chunks):
        one = scatter(
            counts[n][1] * PANEL,
            starts[n],
            theirs[: n + 1],
            [tags_swap] * (n + 1),
            counts[: n + 1],
            own,
            starts[n] * PANEL,
            [last, tags_up] if n == 0 else [last, *came[: n - 1]],
        )
        came.append(lax.ppermute(one, "leaf", up))
        last = one
    pinned = [last, *own_right[:PINNED], *came[:-1]]
    held, update = solve(
        1, theirs, [tags_swap] * chunks, counts, (levels - 1) * sep_panels, right, None, pinned, [], SPLIT
    )
    above_left = above_right = None
    if levels > 2:
        rows = (levels - 2) * sep_cols
        above_right = scatter(rows, sep_panels, mine, [tags] * chunks, counts, [], 0, [])
        above_left = scatter(rows, sep_panels, theirs, [tags_swap] * chunks, counts, [above_right], 0, [])
    for level in range(2, levels + 1):
        span = 2**level
        owners = range(span // 2, leaves, span)
        step = span // 4
        pairs = [[(a - step, a) for a in owners], [(a + step, a) for a in owners]]
        base = (level - 2) * sep_panels
        if level == 2:
            dense, tag_pair = [*came, *own_right], [tags_up, tags_swap]
            own_rows, own_tags, own_counts = mine, [tags] * chunks, counts
        else:
            dense = [lax.ppermute(dense_now, "leaf", one) for one in pairs]
            tag_pair = [lax.ppermute(tags, "leaf", one) for one in pairs]
            own_rows, own_tags, own_counts = [], [], []
        came_update = [lax.ppermute(update, "leaf", one) for one in pairs]
        firsts = [(n_leaf, n_sep)] * 2
        right = right_side(base, own_rows, own_tags, own_counts, dense, [update], BASE_COST)
        if level < levels:
            parts = (above_left, above_right) if level == 2 else (above_now, above_now)
            parts = [lax.ppermute(part, "leaf", one) for part, one in zip(parts, pairs)]
            rows = (levels - level) * sep_cols
            total = scatter(
                rows,
                base + sep_panels,
                [*own_rows, *came_update],
                [*own_tags, *tag_pair],
                [*own_counts, *firsts],
                [sum_two(*parts)],
                0,
                [],
            )
            dense_now, above_now = total[:sep_cols], total[sep_cols:]
        held, update = solve(level, came_update, tag_pair, firsts, base, right, held, [])
    return leaf_solution, held


def solution(mesh):
    placed = (
        P(("leaf", "col"), "row"),
        P("leaf", "col"),
        P("leaf", "col"),
        P("leaf", None),
        P(("leaf", "col"), "row"),
        P("leaf", "col"),
        P("leaf", "col"),
        P("leaf", None),
        P(),
    )
    return jax.shard_map(
        on_device,
        mesh=mesh,
        in_specs=placed,
        out_specs=(P(("leaf", "col"), "row"), P(("leaf", "col"), "row")),
        check_vma=False,
    )
```

```python
import functools

import jax
import jax.numpy as jnp
from jax import lax
from jax.experimental import pallas as pl
from jax.experimental.pallas import tpu as pltpu
from jax.sharding import PartitionSpec as P

PANEL = 128
TILE = 256
TAGS = 128
COPIED = 32
PAD = 8
COST = 1000
CUTS, PARTS = (0, 5, 9, 16), 16
VMEM_MIB = 8
LEAF_COST = 2 * 10**9
SPLIT = 4
RELAY_COSTS = (10**9, 1000, 1000)
BASE_COST = 53 * 10**8
F32 = jnp.float32
BF16 = jnp.bfloat16
ANY = pl.BlockSpec(memory_space=pl.ANY)
VMEM = pl.BlockSpec(memory_space=pltpu.VMEM)
SMEM = pl.BlockSpec(memory_space=pltpu.SMEM)
HBM = pl.BlockSpec(memory_space=pltpu.HBM)


def dot(left, right):
    return jnp.dot(left, right, preferred_element_type=F32)


def call(body, ins, specs, outs, out_specs, scratch=(), after=(), flops=COST, moved=1):
    count, extra = len(ins), len(after)

    def trimmed(*refs):
        body(*refs[:count], *refs[count + extra :])

    return pl.pallas_call(
        trimmed,
        out_shape=outs,
        in_specs=list(specs) + [ANY] * extra,
        out_specs=out_specs,
        scratch_shapes=list(scratch),
        compiler_params=pltpu.CompilerParams(vmem_limit_bytes=VMEM_MIB * 2**20),
        cost_estimate=pl.CostEstimate(flops=flops, bytes_accessed=moved, transcendentals=0),
    )(*ins, *after)


def shape(rows, cols, kind=F32):
    return jax.ShapeDtypeStruct((rows, cols), kind)


def masked_diag(tile):
    rows_here = lax.broadcasted_iota(jnp.int32, tile.shape, 0)
    cols_here = lax.broadcasted_iota(jnp.int32, tile.shape, 1)
    wide = tile.astype(F32)
    wide = jnp.where(rows_here > cols_here, wide, 0.0)
    return jnp.where(rows_here == cols_here, 1.0, wide).astype(BF16)


def lower_rows(read, rhs, tile_idx):
    lo, hi = tile_idx * TILE, (tile_idx + 1) * TILE
    total = dot(masked_diag(read(lo, hi, lo, hi)), rhs[lo:hi])
    if tile_idx:
        total = total + dot(read(lo, hi, 0, lo), rhs[0:lo])
    return total


def key_of(row, levels, sep_panels):
    slot = lax.div(row, jnp.int32(sep_panels))
    zeros = jnp.int32(0)
    for bit_pos in range(1, levels + 1):
        zeros = zeros + jnp.where(slot & (2**bit_pos - 1) == 0, 1, 0)
    return jnp.where(zeros == 0, levels - 1, zeros - 1) * sep_panels + row - slot * sep_panels


def tags_kernel(levels, sep_panels, leaf_rows, sep_rows, tags):
    n_leaf, n_sep = leaf_rows.shape[1], sep_rows.shape[1]
    keys = [key_of(leaf_rows[0, j], levels, sep_panels) for j in range(n_leaf)]
    ranks = [jnp.int32(0)] * n_leaf
    for j in range(n_leaf):
        for i in range(j):
            less = jnp.where(keys[i] < keys[j], 1, 0)
            ranks[j] = ranks[j] + less
            ranks[i] = ranks[i] + 1 - less
    for j in range(n_leaf):
        tags[0, ranks[j]] = keys[j]
        tags[0, n_leaf + n_sep + ranks[j]] = jnp.int32(j)
    for j in range(n_sep):
        tags[0, n_leaf + j] = key_of(sep_rows[0, j], levels, sep_panels)


def diagonal_kernel(piece, inverse, rhs, out):
    right = rhs[...]

    def product(first):
        for t in range(piece // TILE):
            out[t * TILE : (t + 1) * TILE] = lower_rows(lambda a, b, c, d: inverse[first + a : first + b, c:d], right, t)

    @pl.when(lax.axis_index("col") == 0)
    def _():
        product(0)

    @pl.when(lax.axis_index("col") != 0)
    def _():
        product(piece)


def copy_tags_kernel(tags, out):
    for j in range(COPIED):
        out[0, j] = tags[0, j]


def leaf_sum(diag, other):
    return (diag[...] + jnp.where(lax.axis_index("col") == 0, 0.0, other[...])).astype(BF16)


def sum_kernel(diag, other, out, token):
    out[...] = leaf_sum(diag, other)
    token[...] = diag[0:8, 0:128]


def below_kernel(order_at, diag, other, below, tags, keep, send):
    right = leaf_sum(diag, other)
    half = keep.shape[1]
    is_first = lax.axis_index("col") == 0
    for t in range(keep.shape[0] // PANEL):
        source = pl.multiple_of(tags[0, order_at + t] * PANEL, PANEL)
        both = dot(below[pl.ds(source, PANEL)], right)
        left_half, right_half = both[:, :half], both[:, half:]
        keep[t * PANEL : (t + 1) * PANEL] = jnp.where(is_first, left_half, right_half)
        send[t * PANEL : (t + 1) * PANEL] = jnp.where(is_first, right_half, left_half)


def gather_kernel(firsts, keep, there, tags, *outs):
    chunks, owns = outs[: len(firsts)], outs[len(firsts) :]
    for chunk, (first, count) in zip(chunks, firsts):
        at = slice(first * PANEL, (first + count) * PANEL)
        chunk[...] = keep[at] + there[at]
    base = 0
    for own in owns:
        own[...] = jnp.zeros_like(own)
        add_rows(own, base, own.shape[0] // PANEL, chunks, [tags] * len(chunks), firsts, 1)
        base += own.shape[0] // PANEL


def add_rows(out, base, panels, arrays, tags, firsts, sign):
    for array, tag, (tag_at, count) in zip(arrays, tags, firsts):
        for i in range(count):
            place = tag[0, tag_at + i] - base

            @pl.when((place >= 0) & (place < panels))
            def _():
                at = pl.ds(pl.multiple_of(place * PANEL, PANEL), PANEL)
                rows = array[i * PANEL : (i + 1) * PANEL]
                out[at] = out[at] + rows if sign > 0 else out[at] - rows


def scatter_kernel(base, firsts, start, *refs):
    arrays, tags = refs[: len(firsts)], refs[len(firsts) : 2 * len(firsts)]
    dense = refs[2 * len(firsts) : -1]
    out = refs[-1]
    if not dense:
        out[...] = jnp.zeros_like(out)
    at, low, high = 0, start, start + out.shape[0]
    for one in dense:
        first, last = max(low - at, 0), min(high - at, one.shape[0])
        if first < last:
            out[at + first - low : at + last - low] = one[first:last]
        at += one.shape[0]
    add_rows(out, base, out.shape[0] // PANEL, arrays, tags, firsts, 1)


def base_kernel(base, firsts, n_dense, *refs):
    refs = list(refs)
    arrays, tags = refs[: len(firsts)], refs[len(firsts) : 2 * len(firsts)]
    dense = refs[2 * len(firsts) : 2 * len(firsts) + n_dense]
    mine, theirs, out = refs[2 * len(firsts) + n_dense :]
    piece, half = theirs.shape
    is_first = lax.axis_index("col") == 0

    @pl.when(is_first)
    def _():
        out[0:piece] = mine[:, 0:half].astype(F32)
        out[piece : 2 * piece] = theirs[...]

    @pl.when(jnp.logical_not(is_first))
    def _():
        out[0:piece] = theirs[...]
        out[piece : 2 * piece] = mine[:, half : 2 * half].astype(F32)

    at_row = 0
    for one in dense:
        rows = min(one.shape[0], 2 * piece)
        out[at_row : at_row + rows] -= one[0:rows]
        at_row = (at_row + rows) % (2 * piece)
    add_rows(out, base, 2 * piece // PANEL, arrays, tags, firsts, -1)


def residual_kernel(base, firsts, *refs):
    arrays, tags = refs[: len(firsts)], refs[len(firsts) : 2 * len(firsts)]
    right, keep, send, acc = refs[2 * len(firsts) :]
    acc[...] = right[...]
    add_rows(acc, base, acc.shape[0] // PANEL, arrays, tags, firsts, -1)
    piece = keep.shape[0]
    is_first = lax.axis_index("col") == 0

    @pl.when(is_first)
    def _():
        keep[...] = acc[0:piece]
        send[...] = acc[piece : 2 * piece]

    @pl.when(jnp.logical_not(is_first))
    def _():
        keep[...] = acc[piece : 2 * piece]
        send[...] = acc[0:piece]


def across_kernel(mine, theirs, inverse, right, *outs):
    piece, half = mine.shape
    is_first = lax.axis_index("col") == 0
    one, two = mine[...].astype(BF16), theirs[...].astype(BF16)
    right[:, 0:half] = jnp.where(is_first, one, two)
    right[:, half : 2 * half] = jnp.where(is_first, two, one)
    held = right[...]
    per = piece // len(outs)
    for t in range(piece // TILE):
        out, at = outs[t * TILE // per], t * TILE % per
        out[at : at + TILE] = dot(inverse[piece + t * TILE : piece + (t + 1) * TILE], held)


def finish_kernel(plan, *refs):
    refs = list(refs)

    def take(count):
        got = refs[:count]
        del refs[:count]
        return got

    diag = take(1)[0]
    others = take(plan["split"])
    widths = take(1)[0]
    below = take(1)[0] if plan["update"] else None
    before = take(1)[0] if plan["before"] else None
    out = take(1)[0]
    piece, half = out.shape[0], out.shape[1] // 2
    is_first = lax.axis_index("col") == 0
    leaf = lax.axis_index("leaf")
    span = 2 ** plan["level"]
    is_owner = leaf % span == span // 2
    width = widths[leaf - leaf % span + span // 2] - jnp.where(is_first, 0, piece)
    row_ids = lax.broadcasted_iota(jnp.int32, out.shape, 0)
    other = jnp.concatenate([one[...] for one in others], 0)
    total = diag[...] + jnp.where(is_first, 0.0, other)
    sol = jnp.where(row_ids < width, total, 0.0).astype(BF16)
    if plan["update"]:
        keep, *sends = take(1 + plan["split"])
        per = sends[0].shape[0]
        for t in range(0, below.shape[0], TILE):
            both = dot(below[t : t + TILE], sol)
            left_half, right_half = both[:, :half], both[:, half:]
            keep[t : t + TILE] = jnp.where(is_first, left_half, right_half)
            sends[t // per][t % per : t % per + TILE] = jnp.where(is_first, right_half, left_half)

    if before is None:
        out[...] = jnp.where(is_owner, sol, jnp.zeros_like(sol))
    else:
        out[...] = jnp.where(is_owner, sol, before[...])


def sum_two_kernel(one, two, out):
    out[...] = one[...] + two[...]


def sum_parts_kernel(whole, *refs):
    *parts, out, again, token = refs
    token[...] = whole[0:8]
    at = 0
    for part in parts:
        here = slice(at, at + part.shape[0])
        total = whole[here] + part[...]
        out[here] = total
        again[here] = total
        at += part.shape[0]
    out[at:] = jnp.zeros((out.shape[0] - at, out.shape[1]), F32)


def sum_two(one, two):
    return call(sum_two_kernel, (one, two), [VMEM] * 2, shape(*one.shape), VMEM)


def on_device(
    leaf_rhs, leaf_inverse, leaf_below, leaf_rows, sep_rhs, sep_inverse, sep_below, sep_rows, sep_width
):
    leaves = lax.axis_size("leaf")
    levels = leaves.bit_length() - 1
    piece, width_rhs = leaf_rhs.shape
    half = width_rhs // 2
    sep_cols = sep_inverse.shape[0]
    sep_piece = sep_inverse.shape[1]
    sep_panels = sep_cols // PANEL
    n_leaf, n_sep = leaf_rows.shape[1], sep_rows.shape[1]
    col = lax.axis_index("col")
    swap = [(0, 1), (1, 0)]

    bottom = dot(leaf_inverse[piece:], leaf_rhs)
    other = lax.ppermute(bottom, "col", swap)
    tags = call(
        functools.partial(tags_kernel, levels, sep_panels),
        (leaf_rows, sep_rows),
        [SMEM, SMEM],
        shape(1, TAGS, jnp.int32),
        SMEM,
        after=[bottom],
        flops=LEAF_COST,
    )
    diag = call(
        functools.partial(diagonal_kernel, piece),
        (leaf_inverse, leaf_rhs),
        [VMEM, VMEM],
        shape(piece, width_rhs),
        VMEM,
        after=[tags],
        flops=LEAF_COST,
    )

    tags_swap = lax.ppermute(tags, "leaf", [(i, i ^ 1) for i in range(leaves)])
    up = [(a - 1, a) for a in range(2, leaves, 4)]

    rhs_out = jnp.where(col == 0, sep_rhs[:, half:], sep_rhs[:, :half]).astype(F32)
    rhs_theirs = lax.ppermute(rhs_out, "col", swap)

    starts = [n_leaf * part // PARTS for part in CUTS]
    counts = [(a, b - a) for a, b in zip(starts, starts[1:])]
    chunks = len(counts)
    keep, send = call(
        functools.partial(below_kernel, n_leaf + n_sep),
        (diag, other, leaf_below, tags),
        [VMEM] * 3 + [SMEM],
        (shape(n_leaf * PANEL, half),) * 2,
        (VMEM,) * 2,
        after=[rhs_theirs],
    )
    got = call(
        functools.partial(gather_kernel, counts),
        (keep, lax.ppermute(send, "col", swap), tags),
        [VMEM] * 2 + [SMEM],
        (*(shape(count * PANEL, half) for first, count in counts), shape(sep_cols + PAD, half)),
        (VMEM,) * (chunks + 1),
        after=[tags_swap],
    )
    mine, own = list(got[:chunks]), list(got[chunks:])

    theirs = [lax.ppermute(one, "leaf", [(i, i + 1) for i in range(0, leaves, 2)]) for one in mine]

    def scatter(rows, base, arrays, tag_list, firsts, dense, start, after, flops=COST):
        return call(
            functools.partial(scatter_kernel, base, firsts, start),
            (*arrays, *tag_list, *dense),
            [VMEM] * len(arrays) + [SMEM] * len(tag_list) + [VMEM] * len(dense),
            shape(rows, half),
            VMEM,
            after=after,
            flops=flops,
        )

    def right_side(base, arrays, tag_list, firsts, dense, after, flops=COST):
        return call(
            functools.partial(base_kernel, base, firsts, len(dense)),
            (*arrays, *tag_list, *dense, sep_rhs, rhs_theirs),
            [VMEM] * len(arrays) + [SMEM] * len(tag_list) + [VMEM] * (len(dense) + 2),
            shape(sep_cols, half),
            VMEM,
            after=after,
            flops=flops,
        )

    def solve(level, arrays, tag_list, firsts, base, right, before, after, after_across=(), split=1):
        update = level < levels
        keep, send = call(
            functools.partial(residual_kernel, base, firsts),
            (*arrays, *tag_list, right),
            [VMEM] * len(arrays) + [SMEM] * len(tag_list) + [VMEM],
            (shape(sep_piece, half),) * 2,
            (VMEM,) * 2,
            [pltpu.VMEM((sep_cols, half), F32)],
            after=after,
        )
        residual, *across = call(
            across_kernel,
            (keep, lax.ppermute(send, "col", swap), sep_inverse),
            [VMEM] * 3,
            (shape(sep_piece, width_rhs, BF16), *(shape(sep_piece // split, width_rhs),) * split),
            (VMEM,) * (1 + split),
            after=after_across,
        )
        other = [lax.ppermute(one, "col", swap) for one in across]
        diag = call(
            functools.partial(diagonal_kernel, sep_piece),
            (sep_inverse, residual),
            [VMEM] * 2,
            shape(sep_piece, width_rhs),
            VMEM,
        )
        plan = dict(level=level, update=update, before=before is not None, split=split)
        ins = [diag, *other, sep_width]
        outs = [shape(sep_piece, width_rhs, BF16)]
        if update:
            ins.append(sep_below)
            outs += [shape(sep_below.shape[0], half)] + [shape(sep_below.shape[0] // split, half)] * split
        if before is not None:
            ins.append(before)
        got = call(
            functools.partial(finish_kernel, plan),
            ins,
            [VMEM] * (1 + split) + [SMEM] + [VMEM] * (len(ins) - 2 - split),
            tuple(outs),
            (VMEM,) * len(outs),
        )
        if not update:
            return got[0], (None, None)
        there = [lax.ppermute(one, "col", swap) for one in got[2:]]
        rows = got[1].shape[0]
        *total, token = call(
            sum_parts_kernel,
            (got[1], *there),
            [VMEM] * (1 + split),
            (shape(rows + PAD, half), shape(rows, half), shape(8, half)),
            (VMEM,) * 3,
        )
        return got[0], (total, token)

    down = [(i + 1, i) for i in range(2, leaves, 4)]
    own_right = [lax.ppermute(one, "leaf", down) for one in own]
    came = []
    last = own[0]
    for n in range(chunks):
        one = scatter(
            counts[n][1] * PANEL,
            starts[n],
            theirs[: n + 1],
            [tags_swap] * (n + 1),
            counts[: n + 1],
            own,
            starts[n] * PANEL,
            [last, *came[: max(n - 1, 0)]],
            RELAY_COSTS[n],
        )
        came.append(lax.ppermute(one, "leaf", up))
        last = one
        if n == 0:
            right = right_side((levels - 1) * sep_panels, mine, [tags] * chunks, counts, [], own[:1])
            leaf_solution, last = call(
                sum_kernel,
                (diag, other),
                [VMEM] * 2,
                (shape(piece, width_rhs, BF16), shape(8, 128)),
                (VMEM, VMEM),
                after=[right],
            )
    pinned = [last, *came[:-1]]
    held, (update, token) = solve(
        1, theirs, [tags_swap] * chunks, counts, (levels - 1) * sep_panels, right, None, pinned, own_right, SPLIT
    )
    above_left = above_right = None
    if levels > 2:
        rows = (levels - 2) * sep_cols
        above_right = scatter(rows, sep_panels, mine, [tags] * chunks, counts, [], 0, [])
        above_left = scatter(rows, sep_panels, theirs, [tags_swap] * chunks, counts, [above_right], 0, [])
    for level in range(2, levels + 1):
        span = 2**level
        owners = range(span // 2, leaves, span)
        step = span // 4
        pairs = [[(a - step, a) for a in owners], [(a + step, a) for a in owners]]
        base = (level - 2) * sep_panels
        if level == 2:
            dense, tag_pair = [*came, *own_right], [None, tags_swap]
            own_rows, own_tags, own_counts = mine, [tags] * chunks, counts
        else:
            dense = [lax.ppermute(dense_now, "leaf", one) for one in pairs]
            tag_pair = [lax.ppermute(tags, "leaf", one) for one in pairs]
            own_rows, own_tags, own_counts = [], [], []
        came_update = [lax.ppermute(rows, "leaf", one) for rows, one in zip(update, pairs)]
        firsts = [(n_leaf, n_sep)] * 2
        right = right_side(base, own_rows, own_tags, own_counts, dense, [token], BASE_COST)
        if level == 2:
            late = call(copy_tags_kernel, (tags,), [SMEM], shape(1, TAGS, jnp.int32), SMEM, after=[right])
            tag_pair[0] = lax.ppermute(late, "leaf", up)
        if level < levels:
            parts = (above_left, above_right) if level == 2 else (above_now, above_now)
            parts = [lax.ppermute(part, "leaf", one) for part, one in zip(parts, pairs)]
            rows = (levels - level) * sep_cols
            total = scatter(
                rows,
                base + sep_panels,
                [*own_rows, *came_update],
                [*own_tags, *tag_pair],
                [*own_counts, *firsts],
                [sum_two(*parts)],
                0,
                [],
            )
            dense_now, above_now = total[:sep_cols], total[sep_cols:]
        held, (update, token) = solve(level, came_update, tag_pair, firsts, base, right, held, [])
    return leaf_solution, held


def solution(mesh):
    placed = (
        P(("leaf", "col"), "row"),
        P("leaf", "col"),
        P("leaf", "col"),
        P("leaf", None),
        P(("leaf", "col"), "row"),
        P("leaf", "col"),
        P("leaf", "col"),
        P("leaf", None),
        P(),
    )
    return jax.shard_map(
        on_device,
        mesh=mesh,
        in_specs=placed,
        out_specs=(P(("leaf", "col"), "row"), P(("leaf", "col"), "row")),
        check_vma=False,
    )
```

```python
import functools

import jax
import jax.numpy as jnp
from jax import lax
from jax.experimental import pallas as pl
from jax.experimental.pallas import tpu as pltpu
from jax.sharding import PartitionSpec as P

PANEL = 128
TILE = 256
TAGS = 128
COPIED = 32
PAD = 8
COST = 1000
CUTS, PARTS = (0, 5, 9, 16), 16
VMEM_MIB = 8
LEAF_COST = 10**9
SPLIT = 4
RELAY_COSTS = (10**9, 1000, 1000)
BASE_COST = 53 * 10**8
F32 = jnp.float32
BF16 = jnp.bfloat16
ANY = pl.BlockSpec(memory_space=pl.ANY)
VMEM = pl.BlockSpec(memory_space=pltpu.VMEM)
SMEM = pl.BlockSpec(memory_space=pltpu.SMEM)
HBM = pl.BlockSpec(memory_space=pltpu.HBM)


def dot(left, right):
    return jnp.dot(left, right, preferred_element_type=F32)


def call(body, ins, specs, outs, out_specs, scratch=(), after=(), flops=COST, moved=1):
    count, extra = len(ins), len(after)

    def trimmed(*refs):
        body(*refs[:count], *refs[count + extra :])

    return pl.pallas_call(
        trimmed,
        out_shape=outs,
        in_specs=list(specs) + [ANY] * extra,
        out_specs=out_specs,
        scratch_shapes=list(scratch),
        compiler_params=pltpu.CompilerParams(vmem_limit_bytes=VMEM_MIB * 2**20),
        cost_estimate=pl.CostEstimate(flops=flops, bytes_accessed=moved, transcendentals=0),
    )(*ins, *after)


def shape(rows, cols, kind=F32):
    return jax.ShapeDtypeStruct((rows, cols), kind)


def masked_diag(tile):
    rows_here = lax.broadcasted_iota(jnp.int32, tile.shape, 0)
    cols_here = lax.broadcasted_iota(jnp.int32, tile.shape, 1)
    wide = tile.astype(F32)
    wide = jnp.where(rows_here > cols_here, wide, 0.0)
    return jnp.where(rows_here == cols_here, 1.0, wide).astype(BF16)


def lower_rows(read, rhs, tile_idx):
    lo, hi = tile_idx * TILE, (tile_idx + 1) * TILE
    total = dot(masked_diag(read(lo, hi, lo, hi)), rhs[lo:hi])
    if tile_idx:
        total = total + dot(read(lo, hi, 0, lo), rhs[0:lo])
    return total


def key_of(row, levels, sep_panels):
    slot = lax.div(row, jnp.int32(sep_panels))
    zeros = jnp.int32(0)
    for bit_pos in range(1, levels + 1):
        zeros = zeros + jnp.where(slot & (2**bit_pos - 1) == 0, 1, 0)
    return jnp.where(zeros == 0, levels - 1, zeros - 1) * sep_panels + row - slot * sep_panels


def tags_kernel(levels, sep_panels, leaf_rows, sep_rows, tags):
    n_leaf, n_sep = leaf_rows.shape[1], sep_rows.shape[1]
    keys = [key_of(leaf_rows[0, j], levels, sep_panels) for j in range(n_leaf)]
    ranks = [jnp.int32(0)] * n_leaf
    for j in range(n_leaf):
        for i in range(j):
            less = jnp.where(keys[i] < keys[j], 1, 0)
            ranks[j] = ranks[j] + less
            ranks[i] = ranks[i] + 1 - less
    for j in range(n_leaf):
        tags[0, ranks[j]] = keys[j]
        tags[0, n_leaf + n_sep + ranks[j]] = jnp.int32(j)
    for j in range(n_sep):
        tags[0, n_leaf + j] = key_of(sep_rows[0, j], levels, sep_panels)


def diagonal_kernel(piece, inverse, rhs, out):
    right = rhs[...]

    def product(first):
        for t in range(piece // TILE):
            out[t * TILE : (t + 1) * TILE] = lower_rows(lambda a, b, c, d: inverse[first + a : first + b, c:d], right, t)

    @pl.when(lax.axis_index("col") == 0)
    def _():
        product(0)

    @pl.when(lax.axis_index("col") != 0)
    def _():
        product(piece)


def copy_tags_kernel(tags, out):
    for j in range(COPIED):
        out[0, j] = tags[0, j]


def leaf_sum(diag, other):
    return (diag[...] + jnp.where(lax.axis_index("col") == 0, 0.0, other[...])).astype(BF16)


def sum_kernel(diag, other, out, token):
    out[...] = leaf_sum(diag, other)
    token[...] = diag[0:8, 0:128]


def below_kernel(order_at, diag, other, below, tags, keep, send):
    right = leaf_sum(diag, other)
    half = keep.shape[1]
    is_first = lax.axis_index("col") == 0
    for t in range(keep.shape[0] // PANEL):
        source = pl.multiple_of(tags[0, order_at + t] * PANEL, PANEL)
        both = dot(below[pl.ds(source, PANEL)], right)
        left_half, right_half = both[:, :half], both[:, half:]
        keep[t * PANEL : (t + 1) * PANEL] = jnp.where(is_first, left_half, right_half)
        send[t * PANEL : (t + 1) * PANEL] = jnp.where(is_first, right_half, left_half)


def gather_kernel(firsts, keep, there, tags, *outs):
    chunks, owns = outs[: len(firsts)], outs[len(firsts) :]
    for chunk, (first, count) in zip(chunks, firsts):
        at = slice(first * PANEL, (first + count) * PANEL)
        chunk[...] = keep[at] + there[at]
    base = 0
    for own in owns:
        own[...] = jnp.zeros_like(own)
        add_rows(own, base, own.shape[0] // PANEL, chunks, [tags] * len(chunks), firsts, 1)
        base += own.shape[0] // PANEL


def add_rows(out, base, panels, arrays, tags, firsts, sign):
    for array, tag, (tag_at, count) in zip(arrays, tags, firsts):
        for i in range(count):
            place = tag[0, tag_at + i] - base

            @pl.when((place >= 0) & (place < panels))
            def _():
                at = pl.ds(pl.multiple_of(place * PANEL, PANEL), PANEL)
                rows = array[i * PANEL : (i + 1) * PANEL]
                out[at] = out[at] + rows if sign > 0 else out[at] - rows


def scatter_kernel(base, firsts, start, *refs):
    arrays, tags = refs[: len(firsts)], refs[len(firsts) : 2 * len(firsts)]
    dense = refs[2 * len(firsts) : -1]
    out = refs[-1]
    if not dense:
        out[...] = jnp.zeros_like(out)
    at, low, high = 0, start, start + out.shape[0]
    for one in dense:
        first, last = max(low - at, 0), min(high - at, one.shape[0])
        if first < last:
            out[at + first - low : at + last - low] = one[first:last]
        at += one.shape[0]
    add_rows(out, base, out.shape[0] // PANEL, arrays, tags, firsts, 1)


def base_kernel(base, firsts, n_dense, *refs):
    refs = list(refs)
    arrays, tags = refs[: len(firsts)], refs[len(firsts) : 2 * len(firsts)]
    dense = refs[2 * len(firsts) : 2 * len(firsts) + n_dense]
    mine, theirs, out = refs[2 * len(firsts) + n_dense :]
    piece, half = theirs.shape
    is_first = lax.axis_index("col") == 0

    @pl.when(is_first)
    def _():
        out[0:piece] = mine[:, 0:half].astype(F32)
        out[piece : 2 * piece] = theirs[...]

    @pl.when(jnp.logical_not(is_first))
    def _():
        out[0:piece] = theirs[...]
        out[piece : 2 * piece] = mine[:, half : 2 * half].astype(F32)

    at_row = 0
    for one in dense:
        rows = min(one.shape[0], 2 * piece)
        out[at_row : at_row + rows] -= one[0:rows]
        at_row = (at_row + rows) % (2 * piece)
    add_rows(out, base, 2 * piece // PANEL, arrays, tags, firsts, -1)


def residual_kernel(base, firsts, *refs):
    arrays, tags = refs[: len(firsts)], refs[len(firsts) : 2 * len(firsts)]
    right, keep, send, acc = refs[2 * len(firsts) :]
    acc[...] = right[...]
    add_rows(acc, base, acc.shape[0] // PANEL, arrays, tags, firsts, -1)
    piece = keep.shape[0]
    is_first = lax.axis_index("col") == 0

    @pl.when(is_first)
    def _():
        keep[...] = acc[0:piece]
        send[...] = acc[piece : 2 * piece]

    @pl.when(jnp.logical_not(is_first))
    def _():
        keep[...] = acc[piece : 2 * piece]
        send[...] = acc[0:piece]


def across_kernel(mine, theirs, inverse, right, *outs):
    piece, half = mine.shape
    is_first = lax.axis_index("col") == 0
    one, two = mine[...].astype(BF16), theirs[...].astype(BF16)
    right[:, 0:half] = jnp.where(is_first, one, two)
    right[:, half : 2 * half] = jnp.where(is_first, two, one)
    held = right[...]
    per = piece // len(outs)
    for t in range(piece // TILE):
        out, at = outs[t * TILE // per], t * TILE % per
        out[at : at + TILE] = dot(inverse[piece + t * TILE : piece + (t + 1) * TILE], held)


def finish_kernel(plan, *refs):
    refs = list(refs)

    def take(count):
        got = refs[:count]
        del refs[:count]
        return got

    diag = take(1)[0]
    others = take(plan["split"])
    widths = take(1)[0]
    below = take(1)[0] if plan["update"] else None
    before = take(1)[0] if plan["before"] else None
    out = take(1)[0]
    piece, half = out.shape[0], out.shape[1] // 2
    is_first = lax.axis_index("col") == 0
    leaf = lax.axis_index("leaf")
    span = 2 ** plan["level"]
    is_owner = leaf % span == span // 2
    width = widths[leaf - leaf % span + span // 2] - jnp.where(is_first, 0, piece)
    row_ids = lax.broadcasted_iota(jnp.int32, out.shape, 0)
    other = jnp.concatenate([one[...] for one in others], 0)
    total = diag[...] + jnp.where(is_first, 0.0, other)
    sol = jnp.where(row_ids < width, total, 0.0).astype(BF16)
    if plan["update"]:
        keep, *sends = take(1 + plan["split"])
        per = sends[0].shape[0]
        for t in range(0, below.shape[0], TILE):
            both = dot(below[t : t + TILE], sol)
            left_half, right_half = both[:, :half], both[:, half:]
            keep[t : t + TILE] = jnp.where(is_first, left_half, right_half)
            sends[t // per][t % per : t % per + TILE] = jnp.where(is_first, right_half, left_half)

    if before is None:
        out[...] = jnp.where(is_owner, sol, jnp.zeros_like(sol))
    else:
        out[...] = jnp.where(is_owner, sol, before[...])


def sum_two_kernel(one, two, out):
    out[...] = one[...] + two[...]


def sum_parts_kernel(whole, *refs):
    *parts, out, again, token = refs
    token[...] = whole[0:8]
    at = 0
    for part in parts:
        here = slice(at, at + part.shape[0])
        total = whole[here] + part[...]
        out[here] = total
        again[here] = total
        at += part.shape[0]
    out[at:] = jnp.zeros((out.shape[0] - at, out.shape[1]), F32)


def sum_two(one, two):
    return call(sum_two_kernel, (one, two), [VMEM] * 2, shape(*one.shape), VMEM)


def on_device(
    leaf_rhs, leaf_inverse, leaf_below, leaf_rows, sep_rhs, sep_inverse, sep_below, sep_rows, sep_width
):
    leaves = lax.axis_size("leaf")
    levels = leaves.bit_length() - 1
    piece, width_rhs = leaf_rhs.shape
    half = width_rhs // 2
    sep_cols = sep_inverse.shape[0]
    sep_piece = sep_inverse.shape[1]
    sep_panels = sep_cols // PANEL
    n_leaf, n_sep = leaf_rows.shape[1], sep_rows.shape[1]
    col = lax.axis_index("col")
    swap = [(0, 1), (1, 0)]

    bottom = dot(leaf_inverse[piece:], leaf_rhs)
    other = lax.ppermute(bottom, "col", swap)
    tags = call(
        functools.partial(tags_kernel, levels, sep_panels),
        (leaf_rows, sep_rows),
        [SMEM, SMEM],
        shape(1, TAGS, jnp.int32),
        SMEM,
        after=[bottom],
        flops=LEAF_COST,
    )
    diag = call(
        functools.partial(diagonal_kernel, piece),
        (leaf_inverse, leaf_rhs),
        [VMEM, VMEM],
        shape(piece, width_rhs),
        VMEM,
        after=[tags],
        flops=LEAF_COST,
    )

    tags_swap = lax.ppermute(tags, "leaf", [(i, i ^ 1) for i in range(leaves)])
    up = [(a - 1, a) for a in range(2, leaves, 4)]

    rhs_out = jnp.where(col == 0, sep_rhs[:, half:], sep_rhs[:, :half]).astype(F32)
    rhs_theirs = lax.ppermute(rhs_out, "col", swap)

    starts = [n_leaf * part // PARTS for part in CUTS]
    counts = [(a, b - a) for a, b in zip(starts, starts[1:])]
    chunks = len(counts)
    keep, send = call(
        functools.partial(below_kernel, n_leaf + n_sep),
        (diag, other, leaf_below, tags),
        [VMEM] * 3 + [SMEM],
        (shape(n_leaf * PANEL, half),) * 2,
        (VMEM,) * 2,
        after=[rhs_theirs],
    )
    got = call(
        functools.partial(gather_kernel, counts),
        (keep, lax.ppermute(send, "col", swap), tags),
        [VMEM] * 2 + [SMEM],
        (*(shape(count * PANEL, half) for first, count in counts), shape(sep_cols + PAD, half)),
        (VMEM,) * (chunks + 1),
        after=[tags_swap],
    )
    mine, own = list(got[:chunks]), list(got[chunks:])

    theirs = [lax.ppermute(one, "leaf", [(i, i + 1) for i in range(0, leaves, 2)]) for one in mine]

    def scatter(rows, base, arrays, tag_list, firsts, dense, start, after, flops=COST):
        return call(
            functools.partial(scatter_kernel, base, firsts, start),
            (*arrays, *tag_list, *dense),
            [VMEM] * len(arrays) + [SMEM] * len(tag_list) + [VMEM] * len(dense),
            shape(rows, half),
            VMEM,
            after=after,
            flops=flops,
        )

    def right_side(base, arrays, tag_list, firsts, dense, after, flops=COST):
        return call(
            functools.partial(base_kernel, base, firsts, len(dense)),
            (*arrays, *tag_list, *dense, sep_rhs, rhs_theirs),
            [VMEM] * len(arrays) + [SMEM] * len(tag_list) + [VMEM] * (len(dense) + 2),
            shape(sep_cols, half),
            VMEM,
            after=after,
            flops=flops,
        )

    def solve(level, arrays, tag_list, firsts, base, right, before, after, after_across=(), split=1):
        update = level < levels
        keep, send = call(
            functools.partial(residual_kernel, base, firsts),
            (*arrays, *tag_list, right),
            [VMEM] * len(arrays) + [SMEM] * len(tag_list) + [VMEM],
            (shape(sep_piece, half),) * 2,
            (VMEM,) * 2,
            [pltpu.VMEM((sep_cols, half), F32)],
            after=after,
        )
        residual, *across = call(
            across_kernel,
            (keep, lax.ppermute(send, "col", swap), sep_inverse),
            [VMEM] * 3,
            (shape(sep_piece, width_rhs, BF16), *(shape(sep_piece // split, width_rhs),) * split),
            (VMEM,) * (1 + split),
            after=after_across,
        )
        other = [lax.ppermute(one, "col", swap) for one in across]
        diag = call(
            functools.partial(diagonal_kernel, sep_piece),
            (sep_inverse, residual),
            [VMEM] * 2,
            shape(sep_piece, width_rhs),
            VMEM,
        )
        plan = dict(level=level, update=update, before=before is not None, split=split)
        ins = [diag, *other, sep_width]
        outs = [shape(sep_piece, width_rhs, BF16)]
        if update:
            ins.append(sep_below)
            outs += [shape(sep_below.shape[0], half)] + [shape(sep_below.shape[0] // split, half)] * split
        if before is not None:
            ins.append(before)
        got = call(
            functools.partial(finish_kernel, plan),
            ins,
            [VMEM] * (1 + split) + [SMEM] + [VMEM] * (len(ins) - 2 - split),
            tuple(outs),
            (VMEM,) * len(outs),
        )
        if not update:
            return got[0], (None, None)
        there = [lax.ppermute(one, "col", swap) for one in got[2:]]
        rows = got[1].shape[0]
        *total, token = call(
            sum_parts_kernel,
            (got[1], *there),
            [VMEM] * (1 + split),
            (shape(rows + PAD, half), shape(rows, half), shape(8, half)),
            (VMEM,) * 3,
        )
        return got[0], (total, token)

    down = [(i + 1, i) for i in range(2, leaves, 4)]
    own_right = [lax.ppermute(one, "leaf", down) for one in own]
    came = []
    last = own[0]
    for n in range(chunks):
        one = scatter(
            counts[n][1] * PANEL,
            starts[n],
            theirs[: n + 1],
            [tags_swap] * (n + 1),
            counts[: n + 1],
            own,
            starts[n] * PANEL,
            [last, *came[: max(n - 1, 0)]],
            RELAY_COSTS[n],
        )
        came.append(lax.ppermute(one, "leaf", up))
        last = one
        if n == 0:
            right = right_side((levels - 1) * sep_panels, mine, [tags] * chunks, counts, [], own[:1])
            leaf_solution, last = call(
                sum_kernel,
                (diag, other),
                [VMEM] * 2,
                (shape(piece, width_rhs, BF16), shape(8, 128)),
                (VMEM, VMEM),
                after=[right],
            )
    pinned = [last, *came[:-1]]
    held, (update, token) = solve(
        1, theirs, [tags_swap] * chunks, counts, (levels - 1) * sep_panels, right, None, pinned, own_right, SPLIT
    )
    above_left = above_right = None
    if levels > 2:
        rows = (levels - 2) * sep_cols
        above_right = scatter(rows, sep_panels, mine, [tags] * chunks, counts, [], 0, [])
        above_left = scatter(rows, sep_panels, theirs, [tags_swap] * chunks, counts, [above_right], 0, [])
    for level in range(2, levels + 1):
        span = 2**level
        owners = range(span // 2, leaves, span)
        step = span // 4
        pairs = [[(a - step, a) for a in owners], [(a + step, a) for a in owners]]
        base = (level - 2) * sep_panels
        if level == 2:
            dense, tag_pair = [*came, *own_right], [None, tags_swap]
            own_rows, own_tags, own_counts = mine, [tags] * chunks, counts
        else:
            dense = [lax.ppermute(dense_now, "leaf", one) for one in pairs]
            tag_pair = [lax.ppermute(tags, "leaf", one) for one in pairs]
            own_rows, own_tags, own_counts = [], [], []
        came_update = [lax.ppermute(rows, "leaf", one) for rows, one in zip(update, pairs)]
        firsts = [(n_leaf, n_sep)] * 2
        right = right_side(base, own_rows, own_tags, own_counts, dense, [token], BASE_COST)
        if level == 2:
            late = call(copy_tags_kernel, (tags,), [SMEM], shape(1, TAGS, jnp.int32), SMEM, after=[right])
            tag_pair[0] = lax.ppermute(late, "leaf", up)
        if level < levels:
            parts = (above_left, above_right) if level == 2 else (above_now, above_now)
            parts = [lax.ppermute(part, "leaf", one) for part, one in zip(parts, pairs)]
            rows = (levels - level) * sep_cols
            total = scatter(
                rows,
                base + sep_panels,
                [*own_rows, *came_update],
                [*own_tags, *tag_pair],
                [*own_counts, *firsts],
                [sum_two(*parts)],
                0,
                [],
            )
            dense_now, above_now = total[:sep_cols], total[sep_cols:]
        held, (update, token) = solve(level, came_update, tag_pair, firsts, base, right, held, [])
    return leaf_solution, held


def solution(mesh):
    placed = (
        P(("leaf", "col"), "row"),
        P("leaf", "col"),
        P("leaf", "col"),
        P("leaf", None),
        P(("leaf", "col"), "row"),
        P("leaf", "col"),
        P("leaf", "col"),
        P("leaf", None),
        P(),
    )
    return jax.shard_map(
        on_device,
        mesh=mesh,
        in_specs=placed,
        out_specs=(P(("leaf", "col"), "row"), P(("leaf", "col"), "row")),
        check_vma=False,
    )
```
